32 devices in a mesh: dp: 16 (over z, x, core), fsdp: 2 (over y).
Axes of the slice: x: 2, y: 2, z: 4, core: 2. Of those that a mesh axis runs over, the one named last changes fastest.
Arguments:
- tokens: bfloat16 [32768, 576], P(('dp', 'fsdp')), may hold values from -6 to 6
- segments: int32 [32768], P(('dp', 'fsdp')), may hold values from 0 to 32, never falling along the last dimension, each value on 1 to 2000 neighbouring positions
- w_query: bfloat16 [576, 576], P('fsdp'), may hold values from -0.25 to 0.25
- w_key: bfloat16 [576, 192], P('fsdp'), may hold values from -0.25 to 0.25
- w_value: bfloat16 [576, 192], P('fsdp'), may hold values from -0.25 to 0.25
- w_out: bfloat16 [576, 576], P('fsdp'), may hold values from -2 to 2
- w_gate: bfloat16 [576, 1536], P('fsdp'), may hold values from -0.25 to 0.25
- w_up: bfloat16 [576, 1536], P('fsdp'), may hold values from -0.25 to 0.25
- w_down: bfloat16 [1536, 576], P('fsdp'), may hold values from -0.15625 to 0.15625
- gain_attn: bfloat16 [576], P('fsdp'), may hold values from 0.25 to 1.75
- gain_ffn: bfloat16 [576], P('fsdp'), may hold values from 0.25 to 1.75
- cotangent: bfloat16 [32768, 576], P(('dp', 'fsdp')), may hold values from -6 to 6
Outputs:
- output: bfloat16 [32768, 576], P(('dp', 'fsdp'))
- grad_tokens: bfloat16 [32768, 576], P(('dp', 'fsdp'))
- grad_query: float32 [576, 576], P('fsdp')
- grad_key: float32 [576, 192], P('fsdp')
- grad_value: float32 [576, 192], P('fsdp')
- grad_out: float32 [576, 576], P('fsdp')
- grad_gate: float32 [576, 1536], P('fsdp')
- grad_up: float32 [576, 1536], P('fsdp')
- grad_down: float32 [1536, 576], P('fsdp')
- grad_gain_attn: float32 [576], P('fsdp')
- grad_gain_ffn: float32 [576], P('fsdp')
The draws below stay inside these ranges and needn't reach their ends.
Inputs may be any that keep to these rules, and one draw needn't show every extreme that they name: `segments`: segment numbers never fall along the tokens; a document has at most 2000 tokens, and one has exactly 2000.
All inputs are finite; a program needn't handle non-finite values.
Results may differ from the reference program's by a relative error of at most 0.014.
Values may be sent and summed in bfloat16 or wider, within the bound.
A program may use at most 192 MiB of HBM per device.

```python
import math
from functools import partial
import jax
import jax.numpy as jnp
import numpy as np
from jax import lax

D = 576
FF = 1536
HEADS = 9
KV_HEADS = 3
HEAD_DIM = 64
SEQ = 1024
DOC_MOST = 2000
KVW = 192
TOKENS = 32768
DOCUMENTS = 33


def shard_levels(own_key, extent, shards, low, high):
    level = 1.0
    for axis_at, shards_of in shards:
        draws = jax.random.uniform(jax.random.fold_in(jax.random.fold_in(own_key, 6), axis_at), (shards_of,), jnp.float32, low / len(shards), high / len(shards))
        level = level * jnp.repeat(jnp.exp(draws), extent[axis_at] // shards_of).reshape((-1,) + (1,) * (len(extent) - 1 - axis_at))
    return level


def length_profile(number_of, total, most, skew):
    weights = [(1 << 20) // math.isqrt(grade ** skew) + 1 for grade in range(2, number_of + 1)]
    spare, counts = total - most - (number_of - 1), [1] * (number_of - 1)
    while spare > 0:
        free = [i for i in range(number_of - 1) if counts[i] < most]
        mass, left = sum([weights[i] for i in free]), spare
        for i in free:
            extra = min(most - counts[i], max(1, left * weights[i] // mass), spare)
            counts[i] = counts[i] + extra
            spare = spare - extra
    return np.array([most] + counts)


def ragged(rng, amount, total, limit, slope):
    if amount == 2:
        one = jax.random.randint(rng, (), max(1, total - limit), min(limit, total - 1) + 1)
        return jnp.stack([one, total - one])
    sizes = jnp.asarray(length_profile(amount, total, limit, slope), jnp.int32)
    couples = (amount - 1) // 2
    giver, taker = sizes[1:1 + 2 * couples:2], sizes[2:2 + 2 * couples:2]
    slack = jnp.minimum(giver - 1, limit - taker)
    shifted = jax.random.randint(jax.random.fold_in(rng, 1), (couples,), 0, 1 << 20) % (slack + 1)
    sizes = sizes.at[1:1 + 2 * couples:2].set(giver - shifted).at[2:2 + 2 * couples:2].set(taker + shifted)
    return sizes[jax.random.permutation(jax.random.fold_in(rng, 2), amount)]


def centred(key, shape, width, reach, cuts=(), kind=jnp.bfloat16):
    drawn = jax.random.normal(key, shape, jnp.float32) * width
    if len(cuts) > 0:
        drawn = shard_levels(key, shape, cuts, -0.22, 0.18) * drawn
    return jnp.clip(drawn, min=-reach, max=reach).astype(kind)


def setup_inputs(seed: int = 0) -> dict:
    seeds = jax.random.split(jax.random.key(seed), 13)
    return {
        "tokens": centred(seeds[0], (TOKENS, D), 1.0, 6.0, ((0, 32),)),
        "segments": jnp.searchsorted(jnp.cumsum(ragged(seeds[1], DOCUMENTS, TOKENS, DOC_MOST, 1)), jnp.arange(TOKENS), side="right").astype(jnp.int32),
        "w_query": centred(seeds[2], (D, D), D ** -0.5, 0.25, ((0, 2),)),
        "w_key": centred(seeds[3], (D, KVW), D ** -0.5, 0.25, ((0, 2),)),
        "w_value": centred(seeds[4], (D, KVW), D ** -0.5, 0.25, ((0, 2),)),
        "w_out": centred(seeds[5], (D, D), (D // 64) ** -0.5, 2.0, ((0, 2),)),
        "w_gate": centred(seeds[6], (D, FF), D ** -0.5, 0.25, ((0, 2),)),
        "w_up": centred(seeds[7], (D, FF), D ** -0.5, 0.25, ((0, 2),)),
        "w_down": centred(seeds[8], (FF, D), FF ** -0.5, 0.15625, ((0, 2),)),
        "gain_attn": jnp.clip(1.0 + 0.15 * jax.random.normal(seeds[9], (D,), jnp.float32), 0.25, 1.75).astype(jnp.bfloat16),
        "gain_ffn": jnp.clip(1.0 + 0.15 * jax.random.normal(seeds[10], (D,), jnp.float32), 0.25, 1.75).astype(jnp.bfloat16),
        "cotangent": centred(seeds[11], (TOKENS, D), 1.0, 6.0, ((0, 32),)),
    }


@jax.custom_vjp
def low(v):
    return lax.optimization_barrier(v.astype(jnp.bfloat16)).astype(jnp.float32)

@jax.custom_vjp
def low_back(v):
    return v

def low_keep(v):
    return (low(v), None)

def low_pass(kept, grad):
    return (grad,)

def back_keep(v):
    return (v, None)

def back_low(kept, grad):
    return (low(grad),)
low.defvjp(low_keep, low_pass)
low_back.defvjp(back_keep, back_low)
epsilon = 1e-05
rope_base = 100000.0
highest = lax.Precision.HIGHEST

def positions_of(segments):
    seq_rows = segments.reshape(-1, SEQ)
    index = jnp.broadcast_to(jnp.arange(SEQ, dtype=jnp.int32), seq_rows.shape)
    starting = jnp.concatenate([jnp.ones((seq_rows.shape[0], 1), dtype=bool), seq_rows[:, 1:] != seq_rows[:, :-1]], axis=1)
    first_index = lax.cummax(jnp.where(starting, index, jnp.zeros_like(index)), axis=1)
    return (index - first_index).reshape(-1)

def angles(positions):
    freqs = rope_base ** (-jnp.arange(0, HEAD_DIM, 2).astype(jnp.float32) / HEAD_DIM)
    phase = positions.astype(jnp.float32)[:, None] * freqs[None, :]
    phase = jnp.concatenate([phase, phase], axis=1)
    return (jnp.cos(phase)[:, None, :], jnp.sin(phase)[:, None, :])

def rotate(field, cosine, sine):
    half_dim = field.shape[-1] // 2
    turned = jnp.concatenate([-field[..., half_dim:], field[..., :half_dim]], axis=-1)
    return field * cosine + turned * sine

def rms_scale(field):
    return lax.rsqrt(lax.optimization_barrier(jnp.mean(field * field, axis=1, keepdims=True)) + epsilon)

def attend_sequence(queries, keys, values, segment_row):
    scale_factor = HEAD_DIM ** (-0.5)
    scores = jnp.einsum('qkgd,skd->kgqs', queries, keys, precision=highest) * scale_factor
    scores = low_back(scores)
    index = jnp.arange(SEQ)
    allowed = (index[:, None] >= index[None, :]) & (segment_row[:, None] == segment_row[None, :])
    masked = jnp.where(allowed, scores, -jnp.inf)
    weights = low(jax.nn.softmax(masked, axis=-1))
    return jnp.einsum('kgqs,skd->qkgd', weights, values, precision=highest)

def forward(segments, tokens, w_query, w_key, w_value, w_out, w_gate, w_up, w_down, gain_attn, gain_ffn):
    count = tokens.shape[0]
    groups = HEADS // KV_HEADS
    cosine, sine = angles(positions_of(segments))
    normed_attn = tokens * rms_scale(tokens)
    hidden_attn = low(normed_attn * gain_attn)
    queries = low_back(jnp.dot(hidden_attn, w_query, precision=highest))
    keys = low_back(jnp.dot(hidden_attn, w_key, precision=highest))
    values = low(low_back(jnp.dot(hidden_attn, w_value, precision=highest)))
    queries = low(rotate(queries.reshape(count, HEADS, HEAD_DIM), cosine, sine))
    keys = low(rotate(keys.reshape(count, KV_HEADS, HEAD_DIM), cosine, sine))
    queries = queries.reshape(-1, SEQ, KV_HEADS, groups, HEAD_DIM)
    keys = keys.reshape(-1, SEQ, KV_HEADS, HEAD_DIM)
    values = values.reshape(-1, SEQ, KV_HEADS, HEAD_DIM)
    seg_rows = segments.reshape(-1, SEQ)
    checked = jax.checkpoint(attend_sequence)
    mixed = lax.map(lambda parts: checked(parts[0], parts[1], parts[2], parts[3]), (queries, keys, values, seg_rows))
    mixed = low(low_back(mixed.reshape(count, D)))
    branch = low_back(jnp.dot(mixed, w_out, precision=highest))
    middle = tokens + branch
    normed_ffn = middle * rms_scale(middle)
    hidden_ffn = low(normed_ffn * gain_ffn)
    gate = low_back(jnp.dot(hidden_ffn, w_gate, precision=highest))
    upward = low_back(jnp.dot(hidden_ffn, w_up, precision=highest))
    inner = low(jax.nn.silu(gate) * upward)
    return middle + low_back(jnp.dot(inner, w_down, precision=highest))

def reference(tokens, segments, w_query, w_key, w_value, w_out, w_gate, w_up, w_down, gain_attn, gain_ffn, cotangent):
    floats = [arr.astype(jnp.float32) for arr in (tokens, w_query, w_key, w_value, w_out, w_gate, w_up, w_down, gain_attn, gain_ffn)]
    output, pullback = jax.vjp(partial(forward, segments), *floats)
    grads = pullback(cotangent.astype(jnp.float32))
    return (output.astype(jnp.bfloat16), grads[0].astype(jnp.bfloat16), grads[1], grads[2], grads[3], grads[4], grads[5], grads[6], grads[7], grads[8], grads[9])
```

```python
import functools

import jax
import jax.numpy as jnp
from jax import lax
from jax.experimental import pallas as pl
from jax.experimental.pallas import tpu as pltpu
from jax.sharding import PartitionSpec as P

D = 576
HEADS = 9
KV_HEADS = 3
HEAD_DIM = 64
HALF = 32
SEQ = 1024
KVW = 192
QKV = 960
BLOCK = 256
BLOCKS = SEQ // BLOCK
PIECES = 16

epsilon = 1e-05
rope_base = 100000.0
f32 = jnp.float32
bf16 = jnp.bfloat16


def positions_of(segments):
    seq_rows = segments.reshape(-1, SEQ)
    index = jnp.broadcast_to(jnp.arange(SEQ, dtype=jnp.int32), seq_rows.shape)
    starting = jnp.concatenate(
        [jnp.ones((seq_rows.shape[0], 1), dtype=bool), seq_rows[:, 1:] != seq_rows[:, :-1]], axis=1
    )
    first_index = lax.cummax(jnp.where(starting, index, jnp.zeros_like(index)), axis=1)
    return (index - first_index).reshape(-1)


def rms_scale(field):
    return lax.rsqrt(jnp.mean(field * field, axis=1, keepdims=True) + epsilon)


def dot_t(a, b):
    return lax.dot_general(a, b, (((0,), (0,)), ((), ())), preferred_element_type=f32)


def mm(a, b):
    return jnp.dot(a, b, preferred_element_type=f32)


def fill_bias(bias_ref, seg_col_ref, seg_row_ref, block):
    wide = (block + 1) * BLOCK
    key_at = lax.broadcasted_iota(jnp.int32, (wide, BLOCK), 0)
    query_at = lax.broadcasted_iota(jnp.int32, (wide, BLOCK), 1) + block * BLOCK
    same = seg_col_ref[0:wide, :] == seg_row_ref[:, block * BLOCK : wide]
    bias_ref[0:wide, :] = jnp.where((key_at <= query_at) & same, 0.0, -1e30)


def forward_kernel(
    raw_ref, cos_ref, sin_ref, seg_col_ref, seg_row_ref,
    query_ref, key_ref, value_ref, mixed_ref, lse_ref, bias_ref, key_nat_ref,
):
    cosine, sine = cos_ref[...], sin_ref[...]

    def turn(start, scale):
        low = raw_ref[start : start + HALF, :] * scale
        high = raw_ref[start + HALF : start + HEAD_DIM, :] * scale
        return jnp.concatenate(
            [low * cosine - high * sine, high * cosine + low * sine], axis=0
        ).astype(bf16)

    for head in range(HEADS):
        query_ref[head] = turn(head * HEAD_DIM, HEAD_DIM ** (-0.5))
    for head in range(KV_HEADS):
        key = turn(D + head * HEAD_DIM, 1.0)
        key_ref[head] = key
        key_nat_ref[head] = key.T
        start = D + KVW + head * HEAD_DIM
        value_ref[head] = raw_ref[start : start + HEAD_DIM, :].astype(bf16)

    for block in range(BLOCKS):
        wide = (block + 1) * BLOCK
        columns = slice(block * BLOCK, wide)
        fill_bias(bias_ref, seg_col_ref, seg_row_ref, block)

        def one_kv(kv, _):
            for group in range(HEADS // KV_HEADS):
                head = kv * (HEADS // KV_HEADS) + group
                scores = mm(key_nat_ref[kv, 0:wide, :], query_ref[head, :, columns])
                scores = scores + bias_ref[0:wide, :]
                top = jnp.max(scores, axis=0, keepdims=True)
                expd = jnp.exp(scores - top)
                total = jnp.sum(expd, axis=0, keepdims=True)
                mixed = mm(value_ref[kv, :, 0:wide], expd.astype(bf16))
                mixed_ref[head, :, columns] = (mixed / total).astype(bf16)
                lse_ref[head, :, columns] = top + jnp.log(total)
            return 0

        lax.fori_loop(0, KV_HEADS, one_kv, 0)


def backward_kernel(
    query_ref, key_ref, value_ref, mixed_ref, lse_ref, grad_ref, cos_ref, sin_ref,
    seg_col_ref, seg_row_ref, out_ref,
    bias_ref, key_nat_ref, value_nat_ref, query_nat_ref, grad_nat_ref, gq_ref, gk_ref, gv_ref,
):
    for head in range(HEADS):
        query_nat_ref[head] = query_ref[head].T
        grad_nat_ref[head] = grad_ref[head].T
    for head in range(KV_HEADS):
        key_nat_ref[head] = key_ref[head].T
        value_nat_ref[head] = value_ref[head].T
    gk_ref[...] = jnp.zeros_like(gk_ref)
    gv_ref[...] = jnp.zeros_like(gv_ref)

    for block in range(BLOCKS):
        wide = (block + 1) * BLOCK
        columns = slice(block * BLOCK, wide)
        fill_bias(bias_ref, seg_col_ref, seg_row_ref, block)

        def one_kv(kv, _):
            for group in range(HEADS // KV_HEADS):
                head = kv * (HEADS // KV_HEADS) + group
                grad = grad_ref[head, :, columns]
                delta = jnp.sum(
                    grad.astype(f32) * mixed_ref[head, :, columns].astype(f32), axis=0, keepdims=True
                )
                scores = mm(key_nat_ref[kv, 0:wide, :], query_ref[head, :, columns])
                prob = jnp.exp(scores + bias_ref[0:wide, :] - lse_ref[head, :, columns])
                gv_ref[kv, 0:wide, :] += mm(prob.astype(bf16), grad_nat_ref[head, columns, :])
                g_prob = mm(value_nat_ref[kv, 0:wide, :], grad)
                g_score = (prob * (g_prob - delta)).astype(bf16)
                gk_ref[kv, 0:wide, :] += mm(g_score, query_nat_ref[head, columns, :])
                gq_ref[head, :, columns] = mm(key_ref[kv, :, 0:wide], g_score)
            return 0

        lax.fori_loop(0, KV_HEADS, one_kv, 0)

    cosine, sine = cos_ref[...], sin_ref[...]

    def unturn(field):
        low, high = field[:HALF, :], field[HALF:, :]
        return jnp.concatenate(
            [low * cosine + high * sine, high * cosine - low * sine], axis=0
        ).astype(bf16)

    for head in range(HEADS):
        out_ref[head] = unturn(gq_ref[head] * HEAD_DIM ** (-0.5))
    for head in range(KV_HEADS):
        out_ref[HEADS + head] = unturn(gk_ref[head].T)
        out_ref[HEADS + KV_HEADS + head] = gv_ref[head].T.astype(bf16)


def vmem(count):
    return [pl.BlockSpec(memory_space=pltpu.VMEM)] * count


def attend_forward(raw, cosine, sine, seg_col, seg_row):
    return pl.pallas_call(
        forward_kernel,
        out_shape=(
            jax.ShapeDtypeStruct((HEADS, HEAD_DIM, SEQ), bf16),
            jax.ShapeDtypeStruct((KV_HEADS, HEAD_DIM, SEQ), bf16),
            jax.ShapeDtypeStruct((KV_HEADS, HEAD_DIM, SEQ), bf16),
            jax.ShapeDtypeStruct((HEADS, HEAD_DIM, SEQ), bf16),
            jax.ShapeDtypeStruct((HEADS, 1, SEQ), f32),
        ),
        in_specs=vmem(5),
        out_specs=tuple(vmem(5)),
        scratch_shapes=[
            pltpu.VMEM((SEQ, BLOCK), f32),
            pltpu.VMEM((KV_HEADS, SEQ, HEAD_DIM), bf16),
        ],
        compiler_params=pltpu.CompilerParams(vmem_limit_bytes=40 << 20),
        cost_estimate=pl.CostEstimate(
            flops=16_000_000_000, bytes_accessed=9_000_000, transcendentals=6_000_000
        ),
    )(raw, cosine, sine, seg_col, seg_row)


def attend_backward(query, key, value, mixed, lse, grad, cosine, sine, seg_col, seg_row):
    nat = lambda heads, kind: pltpu.VMEM((heads, SEQ, HEAD_DIM), kind)
    return pl.pallas_call(
        backward_kernel,
        out_shape=jax.ShapeDtypeStruct((HEADS + 2 * KV_HEADS, HEAD_DIM, SEQ), bf16),
        in_specs=vmem(10),
        out_specs=vmem(1)[0],
        scratch_shapes=[
            pltpu.VMEM((SEQ, BLOCK), f32),
            nat(KV_HEADS, bf16),
            nat(KV_HEADS, bf16),
            nat(HEADS, bf16),
            nat(HEADS, bf16),
            pltpu.VMEM((HEADS, HEAD_DIM, SEQ), f32),
            nat(KV_HEADS, f32),
            nat(KV_HEADS, f32),
        ],
        compiler_params=pltpu.CompilerParams(vmem_limit_bytes=48 << 20),
        cost_estimate=pl.CostEstimate(
            flops=40_000_000_000, bytes_accessed=9_000_000, transcendentals=6_000_000
        ),
    )(query, key, value, mixed, lse, grad, cosine, sine, seg_col, seg_row)


def swap(field, axis, size, bit):
    return lax.ppermute(field, axis, [(i, i ^ bit) for i in range(size)])


def gather_pair(shard, dp, dp_size):
    half = shard.shape[0] // 2
    core = dp % 2
    mine = lax.dynamic_slice_in_dim(shard, core * half, half)
    got = swap(mine, "fsdp", 2, 1)
    rest = swap(got, "dp", dp_size, 1)
    other = jnp.where(core == 0, jnp.concatenate([got, rest]), jnp.concatenate([rest, got]))
    return other


def gather_full(shard, dp, fs, sizes):
    if sizes[1] == 2 and sizes[0] % 2 == 0:
        other = gather_pair(shard, dp, sizes[0])
        return jnp.where(fs == 0, jnp.concatenate([shard, other]), jnp.concatenate([other, shard]))
    return lax.all_gather(shard, "fsdp", axis=0, tiled=True)


def take_half(field, at):
    keep = lax.dynamic_index_in_dim(field, at, 0, keepdims=False)
    send = lax.dynamic_index_in_dim(field, 1 - at, 0, keepdims=False)
    return keep, send


def reduce_pieces(field, dp, fs, sizes):
    add = lambda a, b: (a.astype(f32) + b.astype(f32)).astype(bf16)
    rows, columns = field.shape[2:]
    n = sizes[0]
    bits = [1 << k for k in range(n.bit_length() - 1)]
    halved = bits[:4]
    cur = field.reshape(sizes[1], 2, PIECES // 2, rows, columns).swapaxes(0, 1)
    keep, send = take_half(cur, dp % 2)
    cur = add(keep, swap(send, "dp", n, 1))
    if sizes[1] == 2:
        keep, send = take_half(cur, fs)
        cur = add(keep, swap(send, "fsdp", 2, 1))
    else:
        cur = lax.psum_scatter(cur, "fsdp", scatter_dimension=0, tiled=False)
    for bit in halved[1:]:
        cur = cur.reshape(2, cur.shape[0] // 2, rows, columns)
        keep, send = take_half(cur, (dp // bit) % 2)
        cur = add(keep, swap(send, "dp", n, bit))
    for bit in bits[4:]:
        cur = add(cur, swap(cur, "dp", n, bit))
    for bit in halved[::-1]:
        other = swap(cur, "dp", n, bit)
        at = (dp // bit) % 2
        cur = jnp.where(at == 0, jnp.concatenate([cur, other]), jnp.concatenate([other, cur]))
    return cur


def as_pieces(field, shares, rows_by, columns_by):
    total, columns = field.shape
    rows = total // shares
    cut = field.reshape(shares, rows_by, rows // rows_by, columns_by, columns // columns_by)
    return cut.transpose(0, 1, 3, 2, 4).reshape(
        shares, rows_by * columns_by, rows // rows_by, columns // columns_by
    )


def from_pieces(field, rows_by, columns_by):
    _, rows, columns = field.shape
    cut = field.reshape(rows_by, columns_by, rows, columns).transpose(0, 2, 1, 3)
    return cut.reshape(rows_by * rows, columns_by * columns)


def on_device(
    sizes,
    tokens,
    segments,
    w_query,
    w_key,
    w_value,
    w_out,
    w_gate,
    w_up,
    w_down,
    gain_attn,
    gain_ffn,
    cotangent,
):
    dp, fs = lax.axis_index("dp"), lax.axis_index("fsdp")
    count = tokens.shape[0]
    seq_count = count // SEQ
    shard_d = w_query.shape[0]

    gains = jnp.concatenate(
        [gain_attn[:, None], gain_ffn[:, None], jnp.zeros((shard_d, 62), bf16)], axis=1
    )
    first = jnp.concatenate([w_query, w_key, w_value, gains], axis=1)
    first_full = gather_full(first, dp, fs, sizes)
    w_qkv = first_full[:, :QKV]
    ga_full = first_full[:, QKV].astype(f32)
    gf_full = first_full[:, QKV + 1].astype(f32)
    later, _ = lax.optimization_barrier(((w_out, w_gate, w_up, w_down), first_full))
    wo_full, wg_full, wu_full, wd_full = [gather_full(w, dp, fs, sizes) for w in later]

    positions = positions_of(segments)
    freqs = rope_base ** (-jnp.arange(0, HEAD_DIM, 2).astype(f32) / HEAD_DIM)
    phase = freqs[:, None] * positions.astype(f32)[None, :]
    cosine, sine = jnp.cos(phase), jnp.sin(phase)

    tok_float = tokens.astype(f32)
    scale_attn = rms_scale(tok_float)
    normed_attn = tok_float * scale_attn
    hidden_attn = (normed_attn * ga_full).astype(bf16)
    raw = lax.dot_general(
        w_qkv, hidden_attn, (((0,), (1,)), ((), ())), preferred_element_type=f32
    )
    spans = [slice(s * SEQ, (s + 1) * SEQ) for s in range(seq_count)]
    seg_cols = [segments[span].reshape(SEQ, 1) for span in spans]
    seg_rows = [segments[span].reshape(1, SEQ) for span in spans]
    kept = [
        attend_forward(raw[:, span], cosine[:, span], sine[:, span], col, row)
        for span, col, row in zip(spans, seg_cols, seg_rows)
    ]
    join = lambda parts: parts[0] if len(parts) == 1 else jnp.concatenate(parts, axis=-1)
    mixed = join([part[3].reshape(D, SEQ) for part in kept])
    middle = tok_float + dot_t(mixed, wo_full)
    scale_ffn = rms_scale(middle)
    normed_ffn = middle * scale_ffn
    hidden_ffn = (normed_ffn * gf_full).astype(bf16)
    gate = mm(hidden_ffn, wg_full)
    upward = mm(hidden_ffn, wu_full)
    sigmoid_gate = jax.nn.sigmoid(gate)
    silu_gate = gate * sigmoid_gate
    inner = (silu_gate * upward).astype(bf16)
    output = (middle + mm(inner, wd_full)).astype(bf16)

    grad_down = dot_t(inner, cotangent).astype(bf16)
    grad_inner = jnp.einsum("td,fd->tf", cotangent, wd_full, preferred_element_type=f32)
    grad_gate_act = (
        grad_inner * upward * sigmoid_gate * (1.0 + gate * (1.0 - sigmoid_gate))
    ).astype(bf16)
    grad_upward = (grad_inner * silu_gate).astype(bf16)
    grad_gate = dot_t(hidden_ffn, grad_gate_act).astype(bf16)
    grad_up = dot_t(hidden_ffn, grad_upward).astype(bf16)
    grad_hidden_ffn = jnp.einsum(
        "tf,df->td", grad_gate_act, wg_full, preferred_element_type=f32
    ) + jnp.einsum("tf,df->td", grad_upward, wu_full, preferred_element_type=f32)
    grad_gain_ffn = jnp.sum(grad_hidden_ffn * normed_ffn, axis=0)
    grad_normed_ffn = grad_hidden_ffn * gf_full
    grad_middle = cotangent.astype(f32) + scale_ffn * (
        grad_normed_ffn - normed_ffn * jnp.mean(grad_normed_ffn * normed_ffn, axis=1, keepdims=True)
    )
    grad_branch = grad_middle.astype(bf16)

    reduce = functools.partial(reduce_pieces, dp=dp, fs=fs, sizes=sizes)
    pieces = lambda field, *by: as_pieces(field, sizes[1], *by)
    gate_up = jnp.concatenate([pieces(grad_gate, 2, 4), pieces(grad_up, 2, 4)], axis=1)
    gate_up_sum = reduce(gate_up)
    down_sum = reduce(pieces(grad_down, PIECES, 1))

    grad_out = mm(mixed, grad_branch)
    grad_mixed = lax.dot_general(
        wo_full, grad_branch, (((1,), (1,)), ((), ())), preferred_element_type=f32
    ).astype(bf16)
    grad_raw = join(
        [
            attend_backward(
                *part, grad_mixed[:, span].reshape(HEADS, HEAD_DIM, SEQ),
                cosine[:, span], sine[:, span], col, row,
            ).reshape(QKV, SEQ)
            for part, span, col, row in zip(kept, spans, seg_cols, seg_rows)
        ]
    )
    grad_qkv = lax.dot_general(
        hidden_attn, grad_raw, (((0,), (1,)), ((), ())), preferred_element_type=f32
    )
    grad_hidden_attn = lax.dot_general(
        grad_raw, w_qkv, (((0,), (1,)), ((), ())), preferred_element_type=f32
    )
    grad_gain_attn = jnp.sum(grad_hidden_attn * normed_attn, axis=0)
    grad_normed_attn = grad_hidden_attn * ga_full
    grad_tokens = grad_middle + scale_attn * (
        grad_normed_attn
        - normed_attn * jnp.mean(grad_normed_attn * normed_attn, axis=1, keepdims=True)
    )

    wide = pieces(jnp.concatenate([grad_qkv, grad_out], axis=1).astype(bf16), 4, 4)
    slim = jnp.stack([grad_gain_attn, grad_gain_ffn]).reshape(2, sizes[1], shard_d).swapaxes(0, 1)
    slim = slim.reshape(sizes[1], PIECES, 1, 2 * shard_d // PIECES).astype(bf16)
    slim = jnp.pad(slim, ((0, 0), (0, 0), (0, 7), (0, wide.shape[3] - slim.shape[3])))
    attn_sum = reduce(jnp.concatenate([wide, slim], axis=2))
    rows = wide.shape[2]
    wide_sum = from_pieces(attn_sum[:, :rows], 4, 4).astype(f32)
    slim_sum = attn_sum[:, rows, : 2 * shard_d // PIECES].reshape(2, shard_d).astype(f32)

    return (
        output,
        grad_tokens.astype(bf16),
        wide_sum[:, :D],
        wide_sum[:, D : D + KVW],
        wide_sum[:, D + KVW : QKV],
        wide_sum[:, QKV:],
        from_pieces(gate_up_sum[: PIECES // 2], 2, 4).astype(f32),
        from_pieces(gate_up_sum[PIECES // 2 :], 2, 4).astype(f32),
        from_pieces(down_sum, PIECES, 1).astype(f32),
        slim_sum[0],
        slim_sum[1],
    )


def solution(mesh):
    rows, whole = P(("dp", "fsdp"), None), P(("dp", "fsdp"))
    weight, gain = P("fsdp", None), P("fsdp")
    in_specs = (rows, whole) + (weight,) * 7 + (gain, gain, rows)
    out_specs = (rows, rows) + (weight,) * 7 + (gain, gain)
    sizes = (mesh.shape["dp"], mesh.shape["fsdp"])
    return jax.shard_map(
        functools.partial(on_device, sizes),
        mesh=mesh,
        in_specs=in_specs,
        out_specs=out_specs,
        check_vma=False,
    )
```

```python
import functools

import jax
import jax.numpy as jnp
from jax import lax
from jax.experimental import pallas as pl
from jax.experimental.pallas import tpu as pltpu
from jax.sharding import PartitionSpec as P

D = 576
HEADS = 9
KV_HEADS = 3
HEAD_DIM = 64
HALF = 32
SEQ = 1024
KVW = 192
QKV = 960
BLOCK = 256
BLOCKS = SEQ // BLOCK
PIECES = 16

epsilon = 1e-05
rope_base = 100000.0
f32 = jnp.float32
bf16 = jnp.bfloat16


def positions_of(segments):
    seq_rows = segments.reshape(-1, SEQ)
    index = jnp.broadcast_to(jnp.arange(SEQ, dtype=jnp.int32), seq_rows.shape)
    starting = jnp.concatenate(
        [jnp.ones((seq_rows.shape[0], 1), dtype=bool), seq_rows[:, 1:] != seq_rows[:, :-1]], axis=1
    )
    first_index = lax.cummax(jnp.where(starting, index, jnp.zeros_like(index)), axis=1)
    return (index - first_index).reshape(-1)


def rms_scale(field):
    return lax.rsqrt(jnp.mean(field * field, axis=1, keepdims=True) + epsilon)


def dot_t(a, b):
    return lax.dot_general(a, b, (((0,), (0,)), ((), ())), preferred_element_type=f32)


def mm(a, b):
    return jnp.dot(a, b, preferred_element_type=f32)


def fill_bias(bias_ref, seg_col_ref, seg_row_ref, block):
    wide = (block + 1) * BLOCK
    key_at = lax.broadcasted_iota(jnp.int32, (wide, BLOCK), 0)
    query_at = lax.broadcasted_iota(jnp.int32, (wide, BLOCK), 1) + block * BLOCK
    same = seg_col_ref[0:wide, :] == seg_row_ref[:, block * BLOCK : wide]
    bias_ref[0:wide, :] = jnp.where((key_at <= query_at) & same, 0.0, -1e30)


def forward_kernel(
    raw_ref, cos_ref, sin_ref, seg_col_ref, seg_row_ref,
    query_ref, key_ref, value_ref, mixed_ref, lse_ref, bias_ref, key_nat_ref,
):
    cosine, sine = cos_ref[...], sin_ref[...]

    def turn(start, scale):
        low = raw_ref[start : start + HALF, :] * scale
        high = raw_ref[start + HALF : start + HEAD_DIM, :] * scale
        return jnp.concatenate(
            [low * cosine - high * sine, high * cosine + low * sine], axis=0
        ).astype(bf16)

    for head in range(HEADS):
        query_ref[head] = turn(head * HEAD_DIM, HEAD_DIM ** (-0.5))
    for head in range(KV_HEADS):
        key = turn(D + head * HEAD_DIM, 1.0)
        key_ref[head] = key
        key_nat_ref[head] = key.T
        start = D + KVW + head * HEAD_DIM
        value_ref[head] = raw_ref[start : start + HEAD_DIM, :].astype(bf16)

    for block in range(BLOCKS):
        wide = (block + 1) * BLOCK
        columns = slice(block * BLOCK, wide)
        fill_bias(bias_ref, seg_col_ref, seg_row_ref, block)

        def one_kv(kv, _):
            for group in range(HEADS // KV_HEADS):
                head = kv * (HEADS // KV_HEADS) + group
                scores = mm(key_nat_ref[kv, 0:wide, :], query_ref[head, :, columns])
                scores = scores + bias_ref[0:wide, :]
                top = jnp.max(scores, axis=0, keepdims=True)
                expd = jnp.exp(scores - top)
                total = jnp.sum(expd, axis=0, keepdims=True)
                mixed = mm(value_ref[kv, :, 0:wide], expd.astype(bf16))
                mixed_ref[head, :, columns] = (mixed / total).astype(bf16)
                lse_ref[head, :, columns] = top + jnp.log(total)
            return 0

        lax.fori_loop(0, KV_HEADS, one_kv, 0)


def backward_kernel(
    query_ref, key_ref, value_ref, mixed_ref, lse_ref, grad_ref, cos_ref, sin_ref,
    seg_col_ref, seg_row_ref, out_ref,
    bias_ref, key_nat_ref, value_nat_ref, query_nat_ref, grad_nat_ref, gq_ref, gk_ref, gv_ref,
):
    for head in range(HEADS):
        query_nat_ref[head] = query_ref[head].T
        grad_nat_ref[head] = grad_ref[head].T
    for head in range(KV_HEADS):
        key_nat_ref[head] = key_ref[head].T
        value_nat_ref[head] = value_ref[head].T
    gk_ref[...] = jnp.zeros_like(gk_ref)
    gv_ref[...] = jnp.zeros_like(gv_ref)

    for block in range(BLOCKS):
        wide = (block + 1) * BLOCK
        columns = slice(block * BLOCK, wide)
        fill_bias(bias_ref, seg_col_ref, seg_row_ref, block)

        def one_kv(kv, _):
            for group in range(HEADS // KV_HEADS):
                head = kv * (HEADS // KV_HEADS) + group
                grad = grad_ref[head, :, columns]
                delta = jnp.sum(
                    grad.astype(f32) * mixed_ref[head, :, columns].astype(f32), axis=0, keepdims=True
                )
                scores = mm(key_nat_ref[kv, 0:wide, :], query_ref[head, :, columns])
                prob = jnp.exp(scores + bias_ref[0:wide, :] - lse_ref[head, :, columns])
                gv_ref[kv, 0:wide, :] += mm(prob.astype(bf16), grad_nat_ref[head, columns, :])
                g_prob = mm(value_nat_ref[kv, 0:wide, :], grad)
                g_score = (prob * (g_prob - delta)).astype(bf16)
                gk_ref[kv, 0:wide, :] += mm(g_score, query_nat_ref[head, columns, :])
                gq_ref[head, :, columns] = mm(key_ref[kv, :, 0:wide], g_score)
            return 0

        lax.fori_loop(0, KV_HEADS, one_kv, 0)

    cosine, sine = cos_ref[...], sin_ref[...]

    def unturn(field):
        low, high = field[:HALF, :], field[HALF:, :]
        return jnp.concatenate(
            [low * cosine + high * sine, high * cosine - low * sine], axis=0
        ).astype(bf16)

    for head in range(HEADS):
        out_ref[head] = unturn(gq_ref[head] * HEAD_DIM ** (-0.5))
    for head in range(KV_HEADS):
        out_ref[HEADS + head] = unturn(gk_ref[head].T)
        out_ref[HEADS + KV_HEADS + head] = gv_ref[head].T.astype(bf16)


def vmem(count):
    return [pl.BlockSpec(memory_space=pltpu.VMEM)] * count


def attend_forward(raw, cosine, sine, seg_col, seg_row):
    return pl.pallas_call(
        forward_kernel,
        out_shape=(
            jax.ShapeDtypeStruct((HEADS, HEAD_DIM, SEQ), bf16),
            jax.ShapeDtypeStruct((KV_HEADS, HEAD_DIM, SEQ), bf16),
            jax.ShapeDtypeStruct((KV_HEADS, HEAD_DIM, SEQ), bf16),
            jax.ShapeDtypeStruct((HEADS, HEAD_DIM, SEQ), bf16),
            jax.ShapeDtypeStruct((HEADS, 1, SEQ), f32),
        ),
        in_specs=vmem(5),
        out_specs=tuple(vmem(5)),
        scratch_shapes=[
            pltpu.VMEM((SEQ, BLOCK), f32),
            pltpu.VMEM((KV_HEADS, SEQ, HEAD_DIM), bf16),
        ],
        compiler_params=pltpu.CompilerParams(vmem_limit_bytes=40 << 20),
        cost_estimate=pl.CostEstimate(
            flops=16_000_000_000, bytes_accessed=9_000_000, transcendentals=6_000_000
        ),
    )(raw, cosine, sine, seg_col, seg_row)


def attend_backward(query, key, value, mixed, lse, grad, cosine, sine, seg_col, seg_row):
    nat = lambda heads, kind: pltpu.VMEM((heads, SEQ, HEAD_DIM), kind)
    return pl.pallas_call(
        backward_kernel,
        out_shape=jax.ShapeDtypeStruct((HEADS + 2 * KV_HEADS, HEAD_DIM, SEQ), bf16),
        in_specs=vmem(10),
        out_specs=vmem(1)[0],
        scratch_shapes=[
            pltpu.VMEM((SEQ, BLOCK), f32),
            nat(KV_HEADS, bf16),
            nat(KV_HEADS, bf16),
            nat(HEADS, bf16),
            nat(HEADS, bf16),
            pltpu.VMEM((HEADS, HEAD_DIM, SEQ), f32),
            nat(KV_HEADS, f32),
            nat(KV_HEADS, f32),
        ],
        compiler_params=pltpu.CompilerParams(vmem_limit_bytes=48 << 20),
        cost_estimate=pl.CostEstimate(
            flops=40_000_000_000, bytes_accessed=9_000_000, transcendentals=6_000_000
        ),
    )(query, key, value, mixed, lse, grad, cosine, sine, seg_col, seg_row)


def swap(field, axis, size, bit):
    return lax.ppermute(field, axis, [(i, i ^ bit) for i in range(size)])


def gather_pair(shard, dp, dp_size):
    half = shard.shape[0] // 2
    core = dp % 2
    mine = lax.dynamic_slice_in_dim(shard, core * half, half)
    got = swap(mine, "fsdp", 2, 1)
    rest = swap(got, "dp", dp_size, 1)
    other = jnp.where(core == 0, jnp.concatenate([got, rest]), jnp.concatenate([rest, got]))
    return other


def gather_full(shard, dp, fs, sizes):
    if sizes[1] == 2 and sizes[0] % 2 == 0:
        other = gather_pair(shard, dp, sizes[0])
        return jnp.where(fs == 0, jnp.concatenate([shard, other]), jnp.concatenate([other, shard]))
    return lax.all_gather(shard, "fsdp", axis=0, tiled=True)


def take_half(field, at):
    keep = lax.dynamic_index_in_dim(field, at, 0, keepdims=False)
    send = lax.dynamic_index_in_dim(field, 1 - at, 0, keepdims=False)
    return keep, send


def reduce_pieces(field, dp, fs, sizes):
    add = lambda a, b: (a.astype(f32) + b.astype(f32)).astype(bf16)
    rows, columns = field.shape[2:]
    n = sizes[0]
    bits = [1 << k for k in range(n.bit_length() - 1)]
    halved = bits[:4]
    cur = field.reshape(sizes[1], 2, PIECES // 2, rows, columns).swapaxes(0, 1)
    keep, send = take_half(cur, dp % 2)
    cur = add(keep, swap(send, "dp", n, 1))
    if sizes[1] == 2:
        keep, send = take_half(cur, fs)
        cur = add(keep, swap(send, "fsdp", 2, 1))
    else:
        cur = lax.psum_scatter(cur, "fsdp", scatter_dimension=0, tiled=False)
    for bit in halved[1:]:
        cur = cur.reshape(2, cur.shape[0] // 2, rows, columns)
        keep, send = take_half(cur, (dp // bit) % 2)
        cur = add(keep, swap(send, "dp", n, bit))
    for bit in bits[4:]:
        cur = add(cur, swap(cur, "dp", n, bit))
    for bit in halved[::-1]:
        other = swap(cur, "dp", n, bit)
        at = (dp // bit) % 2
        cur = jnp.where(at == 0, jnp.concatenate([cur, other]), jnp.concatenate([other, cur]))
    return cur


def as_pieces(field, shares, rows_by, columns_by):
    total, columns = field.shape
    rows = total // shares
    cut = field.reshape(shares, rows_by, rows // rows_by, columns_by, columns // columns_by)
    return cut.transpose(0, 1, 3, 2, 4).reshape(
        shares, rows_by * columns_by, rows // rows_by, columns // columns_by
    )


def from_pieces(field, rows_by, columns_by):
    _, rows, columns = field.shape
    cut = field.reshape(rows_by, columns_by, rows, columns).transpose(0, 2, 1, 3)
    return cut.reshape(rows_by * rows, columns_by * columns)


DP_BITS = (1, 2, 4, 8)
ORDERS = ((0, 2, 3, 4), (2, 0, 3, 4), (3, 0, 2, 4), (0, 3, 4, 2))
SHARES = ((80, 384), (64, 384), (48, 576), (80, 384))
STEPS = 5


def stream_shapes(order, share):
    free = [0, 1, 2, 3, 4]
    boxes = []
    for dim in (1,) + order:
        free.remove(dim)
        boxes.append((2,) * len(free) + share)
    return boxes


def sum_kernel(*refs):
    gate_ref, up_ref, down_ref, attn_ref, slim_ref = refs[:5]
    q_out, k_out, v_out, o_out, gate_out, up_out, down_out, slim_out = refs[5:13]
    scratch = list(refs[13:])
    streams = len(ORDERS)
    held, result = scratch[:streams], scratch[streams : 2 * streams]
    boxes = [scratch[2 * streams + s * STEPS :][:STEPS] for s in range(streams)]
    send_sem, recv_sem = scratch[-2:]

    dp, fs = lax.axis_index("dp"), lax.axis_index("fsdp")
    mine = [fs] + [(dp // bit) % 2 for bit in DP_BITS]
    partner = [{"fsdp": 1 - fs}] + [
        {"dp": dp + bit - 2 * bit * own} for bit, own in zip(DP_BITS, mine[1:])
    ]

    barrier = pltpu.get_barrier_semaphore()
    for device in partner:
        pl.semaphore_signal(barrier, inc=1, device_id=device, device_id_type=pl.DeviceIdType.MESH)
    pl.semaphore_wait(barrier, len(partner))

    def copy(stream, step, source, target, dim):
        return pltpu.make_async_remote_copy(
            src_ref=source,
            dst_ref=target,
            send_sem=send_sem.at[stream, step],
            recv_sem=recv_sem.at[stream, step],
            device_id=partner[dim],
            device_id_type=pl.DeviceIdType.MESH,
        )

    def at(order, step, own_of_step):
        index = [slice(None)] * 5
        dims = (1,) + order
        for dim in dims[:step]:
            index[dim] = mine[dim]
        index[dims[step]] = own_of_step
        return tuple(index)

    def halve(stream, step):
        order = ORDERS[stream]
        dim = ((1,) + order)[step]
        index = at(order, step, 1 - mine[dim])
        return copy(stream, step, held[stream].at[index], boxes[stream][step], dim)

    def widen(stream, step):
        order = [dim for dim in ((1,) + ORDERS[stream])[::-1] if dim != 0]
        dim = order[step]
        index = [mine[at_dim] for at_dim in range(1, 5)]
        for done in order[:step]:
            index[done - 1] = slice(None)
        where = result[stream].at[tuple(index)]
        return copy(stream, STEPS + step, where, where, dim)

    def fill(stream):
        for f in range(2):
            for p in range(PIECES):
                c, x, zl, zh = p // 8, (p // 4) % 2, (p // 2) % 2, p % 2
                columns = slice((2 * zl + zh) * 384, (2 * zl + zh + 1) * 384)
                if stream < 2:
                    start = f * 288 + x * 144 + (80 if stream == 1 else 0)
                    source = up_ref if c else gate_ref
                    part = source[start : start + SHARES[stream][0], columns]
                elif stream == 2:
                    part = down_ref[f * 768 + p * 48 : f * 768 + p * 48 + 48, :]
                else:
                    start = f * 288 + (2 * c + x) * 72
                    part = jnp.concatenate(
                        [attn_ref[start : start + 72, columns], slim_ref[f, p]], axis=0
                    ).astype(bf16)
                held[stream][f, c, x, zl, zh] = part

    def empty(stream):
        for p in range(PIECES):
            c, x, zl, zh = p // 8, (p // 4) % 2, (p // 2) % 2, p % 2
            columns = slice((2 * zl + zh) * 384, (2 * zl + zh + 1) * 384)
            if stream == 3 and p % 4 != 0:
                continue
            part = result[stream][c, x, zl, zh].astype(f32)
            if stream < 2:
                start = x * 144 + (80 if stream == 1 else 0)
                target = up_out if c else gate_out
                target[start : start + SHARES[stream][0], columns] = part
            elif stream == 2:
                down_out[p * 48 : p * 48 + 48, :] = part
            else:
                quarters = [result[3][c, x, z // 2, z % 2].astype(f32) for z in range(4)]
                for z in range(4):
                    slim_out[p + z] = quarters[z][72:, :]
                row = jnp.concatenate([quarter[:72, :] for quarter in quarters], axis=1)
                rows = slice((p // 4) * 72, (p // 4) * 72 + 72)
                q_out[rows, :] = row[:, :D]
                k_out[rows, :] = row[:, D : D + KVW]
                v_out[rows, :] = row[:, D + KVW : QKV]
                o_out[rows, :] = row[:, QKV:]

    copies = {}
    for stream in range(streams):
        fill(stream)
        copies[stream] = halve(stream, 0)
        copies[stream].start()
    for step in range(STEPS):
        for stream in range(streams):
            copies[stream].wait()
            order = ORDERS[stream]
            dim = ((1,) + order)[step]
            index = at(order, step, mine[dim])
            total = held[stream][index].astype(f32) + boxes[stream][step][...].astype(f32)
            if step < STEPS - 1:
                held[stream][index] = total.astype(bf16)
                copies[stream] = halve(stream, step + 1)
            else:
                result[stream][tuple(mine[1:])] = total.astype(bf16)
                copies[stream] = widen(stream, 0)
            copies[stream].start()
    for step in range(4):
        for stream in range(streams):
            copies[stream].wait()
            if step < 3:
                copies[stream] = widen(stream, step + 1)
                copies[stream].start()
            else:
                empty(stream)


def sum_all(gate, up, down, attn, slim):
    shapes = [(288, D), (288, KVW), (288, KVW), (288, D), (288, 1536), (288, 1536), (768, D)]
    shapes.append((PIECES, 8, 384))
    scratch = [pltpu.VMEM((2,) * 5 + share, bf16) for share in SHARES]
    scratch += [pltpu.VMEM((2,) * 4 + share, bf16) for share in SHARES]
    for order, share in zip(ORDERS, SHARES):
        scratch += [pltpu.VMEM(box, bf16) for box in stream_shapes(order, share)]
    scratch += [pltpu.SemaphoreType.DMA((len(ORDERS), STEPS + 4))] * 2
    return pl.pallas_call(
        sum_kernel,
        out_shape=tuple(jax.ShapeDtypeStruct(shape, f32) for shape in shapes),
        in_specs=vmem(5),
        out_specs=tuple(vmem(8)),
        scratch_shapes=scratch,
        compiler_params=pltpu.CompilerParams(
            collective_id=0, has_side_effects=True, vmem_limit_bytes=56 << 20
        ),
    )(gate, up, down, attn, slim)


def on_device(
    sizes,
    tokens,
    segments,
    w_query,
    w_key,
    w_value,
    w_out,
    w_gate,
    w_up,
    w_down,
    gain_attn,
    gain_ffn,
    cotangent,
):
    dp, fs = lax.axis_index("dp"), lax.axis_index("fsdp")
    count = tokens.shape[0]
    seq_count = count // SEQ
    shard_d = w_query.shape[0]

    gains = jnp.concatenate(
        [gain_attn[:, None], gain_ffn[:, None], jnp.zeros((shard_d, 62), bf16)], axis=1
    )
    first = jnp.concatenate([w_query, w_key, w_value, gains], axis=1)
    first_full = gather_full(first, dp, fs, sizes)
    w_qkv = first_full[:, :QKV]
    ga_full = first_full[:, QKV].astype(f32)
    gf_full = first_full[:, QKV + 1].astype(f32)
    later, _ = lax.optimization_barrier(((w_out, w_gate, w_up, w_down), first_full))
    wo_full, wg_full, wu_full, wd_full = [gather_full(w, dp, fs, sizes) for w in later]

    positions = positions_of(segments)
    freqs = rope_base ** (-jnp.arange(0, HEAD_DIM, 2).astype(f32) / HEAD_DIM)
    phase = freqs[:, None] * positions.astype(f32)[None, :]
    cosine, sine = jnp.cos(phase), jnp.sin(phase)

    tok_float = tokens.astype(f32)
    scale_attn = rms_scale(tok_float)
    normed_attn = tok_float * scale_attn
    hidden_attn = (normed_attn * ga_full).astype(bf16)
    raw = lax.dot_general(
        w_qkv, hidden_attn, (((0,), (1,)), ((), ())), preferred_element_type=f32
    )
    spans = [slice(s * SEQ, (s + 1) * SEQ) for s in range(seq_count)]
    seg_cols = [segments[span].reshape(SEQ, 1) for span in spans]
    seg_rows = [segments[span].reshape(1, SEQ) for span in spans]
    kept = [
        attend_forward(raw[:, span], cosine[:, span], sine[:, span], col, row)
        for span, col, row in zip(spans, seg_cols, seg_rows)
    ]
    join = lambda parts: parts[0] if len(parts) == 1 else jnp.concatenate(parts, axis=-1)
    mixed = join([part[3].reshape(D, SEQ) for part in kept])
    middle = tok_float + dot_t(mixed, wo_full)
    scale_ffn = rms_scale(middle)
    normed_ffn = middle * scale_ffn
    hidden_ffn = (normed_ffn * gf_full).astype(bf16)
    gate = mm(hidden_ffn, wg_full)
    upward = mm(hidden_ffn, wu_full)
    sigmoid_gate = jax.nn.sigmoid(gate)
    silu_gate = gate * sigmoid_gate
    inner = (silu_gate * upward).astype(bf16)
    output = (middle + mm(inner, wd_full)).astype(bf16)

    grad_down = dot_t(inner, cotangent).astype(bf16)
    grad_inner = jnp.einsum("td,fd->tf", cotangent, wd_full, preferred_element_type=f32)
    grad_gate_act = (
        grad_inner * upward * sigmoid_gate * (1.0 + gate * (1.0 - sigmoid_gate))
    ).astype(bf16)
    grad_upward = (grad_inner * silu_gate).astype(bf16)
    grad_gate = dot_t(hidden_ffn, grad_gate_act).astype(bf16)
    grad_up = dot_t(hidden_ffn, grad_upward).astype(bf16)
    grad_hidden_ffn = jnp.einsum(
        "tf,df->td", grad_gate_act, wg_full, preferred_element_type=f32
    ) + jnp.einsum("tf,df->td", grad_upward, wu_full, preferred_element_type=f32)
    grad_gain_ffn = jnp.sum(grad_hidden_ffn * normed_ffn, axis=0)
    grad_normed_ffn = grad_hidden_ffn * gf_full
    grad_middle = cotangent.astype(f32) + scale_ffn * (
        grad_normed_ffn - normed_ffn * jnp.mean(grad_normed_ffn * normed_ffn, axis=1, keepdims=True)
    )
    grad_branch = grad_middle.astype(bf16)

    grad_out = mm(mixed, grad_branch)
    grad_mixed = lax.dot_general(
        wo_full, grad_branch, (((1,), (1,)), ((), ())), preferred_element_type=f32
    ).astype(bf16)
    grad_raw = join(
        [
            attend_backward(
                *part, grad_mixed[:, span].reshape(HEADS, HEAD_DIM, SEQ),
                cosine[:, span], sine[:, span], col, row,
            ).reshape(QKV, SEQ)
            for part, span, col, row in zip(kept, spans, seg_cols, seg_rows)
        ]
    )
    grad_qkv = lax.dot_general(
        hidden_attn, grad_raw, (((0,), (1,)), ((), ())), preferred_element_type=f32
    )
    grad_hidden_attn = lax.dot_general(
        grad_raw, w_qkv, (((0,), (1,)), ((), ())), preferred_element_type=f32
    )
    grad_gain_attn = jnp.sum(grad_hidden_attn * normed_attn, axis=0)
    grad_normed_attn = grad_hidden_attn * ga_full
    grad_tokens = grad_middle + scale_attn * (
        grad_normed_attn
        - normed_attn * jnp.mean(grad_normed_attn * normed_attn, axis=1, keepdims=True)
    )

    wide = jnp.concatenate([grad_qkv, grad_out], axis=1)
    slim = jnp.stack([grad_gain_attn, grad_gain_ffn]).reshape(2, sizes[1], shard_d).swapaxes(0, 1)
    slim = slim.reshape(sizes[1], PIECES, 1, 2 * shard_d // PIECES)
    slim = jnp.pad(slim, ((0, 0), (0, 0), (0, 7), (0, wide.shape[1] // 4 - slim.shape[3])))
    slim_width = 2 * shard_d // PIECES
    if sizes == (16, 2):
        *sums, slim_sum = sum_all(grad_gate, grad_up, grad_down, wide, slim)
        slim_sum = slim_sum[:, 0, :slim_width].reshape(2, shard_d)
        return (output, grad_tokens.astype(bf16), *sums, slim_sum[0], slim_sum[1])

    pieces = lambda field, *by: as_pieces(field, sizes[1], *by)
    reduce = functools.partial(reduce_pieces, dp=dp, fs=fs, sizes=sizes)
    gate_up_sum = reduce(
        jnp.concatenate([pieces(grad_gate, 2, 4), pieces(grad_up, 2, 4)], axis=1)
    )
    down_sum = reduce(pieces(grad_down, PIECES, 1))
    wide = pieces(wide.astype(bf16), 4, 4)
    attn_sum = reduce(jnp.concatenate([wide, slim.astype(bf16)], axis=2))
    rows = wide.shape[2]
    wide_sum = from_pieces(attn_sum[:, :rows], 4, 4).astype(f32)
    slim_sum = attn_sum[:, rows, :slim_width].reshape(2, shard_d).astype(f32)
    return (
        output,
        grad_tokens.astype(bf16),
        wide_sum[:, :D],
        wide_sum[:, D : D + KVW],
        wide_sum[:, D + KVW : QKV],
        wide_sum[:, QKV:],
        from_pieces(gate_up_sum[: PIECES // 2], 2, 4).astype(f32),
        from_pieces(gate_up_sum[PIECES // 2 :], 2, 4).astype(f32),
        from_pieces(down_sum, PIECES, 1).astype(f32),
        slim_sum[0],
        slim_sum[1],
    )


def solution(mesh):
    rows, whole = P(("dp", "fsdp"), None), P(("dp", "fsdp"))
    weight, gain = P("fsdp", None), P("fsdp")
    in_specs = (rows, whole) + (weight,) * 7 + (gain, gain, rows)
    out_specs = (rows, rows) + (weight,) * 7 + (gain, gain)
    sizes = (mesh.shape["dp"], mesh.shape["fsdp"])
    return jax.shard_map(
        functools.partial(on_device, sizes),
        mesh=mesh,
        in_specs=in_specs,
        out_specs=out_specs,
        check_vma=False,
    )
```

```python
import functools

import jax
import jax.numpy as jnp
from jax import lax
from jax.experimental import pallas as pl
from jax.experimental.pallas import tpu as pltpu
from jax.sharding import PartitionSpec as P

D = 576
HEADS = 9
KV_HEADS = 3
HEAD_DIM = 64
HALF = 32
SEQ = 1024
KVW = 192
QKV = 960
BLOCK = 256
BLOCKS = SEQ // BLOCK
PIECES = 16

epsilon = 1e-05
rope_base = 100000.0
f32 = jnp.float32
bf16 = jnp.bfloat16


def positions_of(segments):
    seq_rows = segments.reshape(-1, SEQ)
    index = jnp.broadcast_to(jnp.arange(SEQ, dtype=jnp.int32), seq_rows.shape)
    starting = jnp.concatenate(
        [jnp.ones((seq_rows.shape[0], 1), dtype=bool), seq_rows[:, 1:] != seq_rows[:, :-1]], axis=1
    )
    first_index = lax.cummax(jnp.where(starting, index, jnp.zeros_like(index)), axis=1)
    return (index - first_index).reshape(-1)


def rms_scale(field):
    return lax.rsqrt(jnp.mean(field * field, axis=1, keepdims=True) + epsilon)


def dot_t(a, b):
    return lax.dot_general(a, b, (((0,), (0,)), ((), ())), preferred_element_type=f32)


def mm(a, b):
    return jnp.dot(a, b, preferred_element_type=f32)


def fill_bias(bias_ref, seg_col_ref, seg_row_ref, block):
    wide = (block + 1) * BLOCK
    key_at = lax.broadcasted_iota(jnp.int32, (wide, BLOCK), 0)
    query_at = lax.broadcasted_iota(jnp.int32, (wide, BLOCK), 1) + block * BLOCK
    same = seg_col_ref[0:wide, :] == seg_row_ref[:, block * BLOCK : wide]
    bias_ref[0:wide, :] = jnp.where((key_at <= query_at) & same, 0.0, -1e30)


def forward_kernel(
    raw_ref, cos_ref, sin_ref, seg_col_ref, seg_row_ref,
    query_ref, key_ref, value_ref, mixed_ref, lse_ref, bias_ref, key_nat_ref,
):
    cosine, sine = cos_ref[...], sin_ref[...]

    def turn(start, scale):
        low = raw_ref[start : start + HALF, :] * scale
        high = raw_ref[start + HALF : start + HEAD_DIM, :] * scale
        return jnp.concatenate(
            [low * cosine - high * sine, high * cosine + low * sine], axis=0
        ).astype(bf16)

    for head in range(HEADS):
        query_ref[head] = turn(head * HEAD_DIM, HEAD_DIM ** (-0.5))
    for head in range(KV_HEADS):
        key = turn(D + head * HEAD_DIM, 1.0)
        key_ref[head] = key
        key_nat_ref[head] = key.T
        start = D + KVW + head * HEAD_DIM
        value_ref[head] = raw_ref[start : start + HEAD_DIM, :].astype(bf16)

    for block in range(BLOCKS):
        wide = (block + 1) * BLOCK
        columns = slice(block * BLOCK, wide)
        fill_bias(bias_ref, seg_col_ref, seg_row_ref, block)

        def one_kv(kv, _):
            for group in range(HEADS // KV_HEADS):
                head = kv * (HEADS // KV_HEADS) + group
                scores = mm(key_nat_ref[kv, 0:wide, :], query_ref[head, :, columns])
                scores = scores + bias_ref[0:wide, :]
                top = jnp.max(scores, axis=0, keepdims=True)
                expd = jnp.exp(scores - top)
                total = jnp.sum(expd, axis=0, keepdims=True)
                mixed = mm(value_ref[kv, :, 0:wide], expd.astype(bf16))
                mixed_ref[head, :, columns] = (mixed / total).astype(bf16)
                lse_ref[head, :, columns] = top + jnp.log(total)
            return 0

        lax.fori_loop(0, KV_HEADS, one_kv, 0)


def backward_kernel(
    query_ref, key_ref, value_ref, mixed_ref, lse_ref, grad_ref, cos_ref, sin_ref,
    seg_col_ref, seg_row_ref, out_ref,
    bias_ref, key_nat_ref, value_nat_ref, query_nat_ref, grad_nat_ref, gq_ref, gk_ref, gv_ref,
    between=None,
):
    for head in range(HEADS):
        query_nat_ref[head] = query_ref[head].T
        grad_nat_ref[head] = grad_ref[head].T
    for head in range(KV_HEADS):
        key_nat_ref[head] = key_ref[head].T
        value_nat_ref[head] = value_ref[head].T
    gk_ref[...] = jnp.zeros_like(gk_ref)
    gv_ref[...] = jnp.zeros_like(gv_ref)

    for block in range(BLOCKS)[::-1]:
        wide = (block + 1) * BLOCK
        columns = slice(block * BLOCK, wide)
        fill_bias(bias_ref, seg_col_ref, seg_row_ref, block)

        def one_kv(kv, _):
            for group in range(HEADS // KV_HEADS):
                head = kv * (HEADS // KV_HEADS) + group
                grad = grad_ref[head, :, columns]
                delta = jnp.sum(
                    grad.astype(f32) * mixed_ref[head, :, columns].astype(f32), axis=0, keepdims=True
                )
                scores = mm(key_nat_ref[kv, 0:wide, :], query_ref[head, :, columns])
                prob = jnp.exp(scores + bias_ref[0:wide, :] - lse_ref[head, :, columns])
                gv_ref[kv, 0:wide, :] += mm(prob.astype(bf16), grad_nat_ref[head, columns, :])
                g_prob = mm(value_nat_ref[kv, 0:wide, :], grad)
                g_score = (prob * (g_prob - delta)).astype(bf16)
                gk_ref[kv, 0:wide, :] += mm(g_score, query_nat_ref[head, columns, :])
                gq_ref[head, :, columns] = mm(key_ref[kv, :, 0:wide], g_score)
            return 0

        if between is None:
            lax.fori_loop(0, KV_HEADS, one_kv, 0)
        else:
            for kv in range(KV_HEADS):
                one_kv(kv, 0)
                between(block, kv)

    cosine, sine = cos_ref[...], sin_ref[...]

    def unturn(field):
        low, high = field[:HALF, :], field[HALF:, :]
        return jnp.concatenate(
            [low * cosine + high * sine, high * cosine - low * sine], axis=0
        ).astype(bf16)

    for head in range(HEADS):
        out_ref[head] = unturn(gq_ref[head] * HEAD_DIM ** (-0.5))
    for head in range(KV_HEADS):
        out_ref[HEADS + head] = unturn(gk_ref[head].T)
        out_ref[HEADS + KV_HEADS + head] = gv_ref[head].T.astype(bf16)


def vmem(count):
    return [pl.BlockSpec(memory_space=pltpu.VMEM)] * count


def attend_forward(raw, cosine, sine, seg_col, seg_row):
    return pl.pallas_call(
        forward_kernel,
        out_shape=(
            jax.ShapeDtypeStruct((HEADS, HEAD_DIM, SEQ), bf16),
            jax.ShapeDtypeStruct((KV_HEADS, HEAD_DIM, SEQ), bf16),
            jax.ShapeDtypeStruct((KV_HEADS, HEAD_DIM, SEQ), bf16),
            jax.ShapeDtypeStruct((HEADS, HEAD_DIM, SEQ), bf16),
            jax.ShapeDtypeStruct((HEADS, 1, SEQ), f32),
        ),
        in_specs=vmem(5),
        out_specs=tuple(vmem(5)),
        scratch_shapes=[
            pltpu.VMEM((SEQ, BLOCK), f32),
            pltpu.VMEM((KV_HEADS, SEQ, HEAD_DIM), bf16),
        ],
        compiler_params=pltpu.CompilerParams(vmem_limit_bytes=40 << 20),
        cost_estimate=pl.CostEstimate(
            flops=16_000_000_000, bytes_accessed=9_000_000, transcendentals=6_000_000
        ),
    )(raw, cosine, sine, seg_col, seg_row)


def backward_scratch():
    nat = lambda heads, kind: pltpu.VMEM((heads, SEQ, HEAD_DIM), kind)
    return [
        pltpu.VMEM((SEQ, BLOCK), f32),
        nat(KV_HEADS, bf16),
        nat(KV_HEADS, bf16),
        nat(HEADS, bf16),
        nat(HEADS, bf16),
        pltpu.VMEM((HEADS, HEAD_DIM, SEQ), f32),
        nat(KV_HEADS, f32),
        nat(KV_HEADS, f32),
    ]


def attend_backward(query, key, value, mixed, lse, grad, cosine, sine, seg_col, seg_row):
    return pl.pallas_call(
        backward_kernel,
        out_shape=jax.ShapeDtypeStruct((HEADS + 2 * KV_HEADS, HEAD_DIM, SEQ), bf16),
        in_specs=vmem(10),
        out_specs=vmem(1)[0],
        scratch_shapes=backward_scratch(),
        compiler_params=pltpu.CompilerParams(vmem_limit_bytes=48 << 20),
        cost_estimate=pl.CostEstimate(
            flops=40_000_000_000, bytes_accessed=9_000_000, transcendentals=6_000_000
        ),
    )(query, key, value, mixed, lse, grad, cosine, sine, seg_col, seg_row)


def swap(field, axis, size, bit):
    return lax.ppermute(field, axis, [(i, i ^ bit) for i in range(size)])


def gather_pair(shard, dp, dp_size):
    half = shard.shape[0] // 2
    core = dp % 2
    mine = lax.dynamic_slice_in_dim(shard, core * half, half)
    got = swap(mine, "fsdp", 2, 1)
    rest = swap(got, "dp", dp_size, 1)
    other = jnp.where(core == 0, jnp.concatenate([got, rest]), jnp.concatenate([rest, got]))
    return other


def gather_full(shard, dp, fs, sizes):
    if sizes[1] == 2 and sizes[0] % 2 == 0:
        other = gather_pair(shard, dp, sizes[0])
        return jnp.where(fs == 0, jnp.concatenate([shard, other]), jnp.concatenate([other, shard]))
    return lax.all_gather(shard, "fsdp", axis=0, tiled=True)


def take_half(field, at):
    keep = lax.dynamic_index_in_dim(field, at, 0, keepdims=False)
    send = lax.dynamic_index_in_dim(field, 1 - at, 0, keepdims=False)
    return keep, send


def reduce_pieces(field, dp, fs, sizes):
    add = lambda a, b: (a.astype(f32) + b.astype(f32)).astype(bf16)
    rows, columns = field.shape[2:]
    n = sizes[0]
    bits = [1 << k for k in range(n.bit_length() - 1)]
    halved = bits[:4]
    cur = field.reshape(sizes[1], 2, PIECES // 2, rows, columns).swapaxes(0, 1)
    keep, send = take_half(cur, dp % 2)
    cur = add(keep, swap(send, "dp", n, 1))
    if sizes[1] == 2:
        keep, send = take_half(cur, fs)
        cur = add(keep, swap(send, "fsdp", 2, 1))
    else:
        cur = lax.psum_scatter(cur, "fsdp", scatter_dimension=0, tiled=False)
    for bit in halved[1:]:
        cur = cur.reshape(2, cur.shape[0] // 2, rows, columns)
        keep, send = take_half(cur, (dp // bit) % 2)
        cur = add(keep, swap(send, "dp", n, bit))
    for bit in bits[4:]:
        cur = add(cur, swap(cur, "dp", n, bit))
    for bit in halved[::-1]:
        other = swap(cur, "dp", n, bit)
        at = (dp // bit) % 2
        cur = jnp.where(at == 0, jnp.concatenate([cur, other]), jnp.concatenate([other, cur]))
    return cur


def as_pieces(field, shares, rows_by, columns_by):
    total, columns = field.shape
    rows = total // shares
    cut = field.reshape(shares, rows_by, rows // rows_by, columns_by, columns // columns_by)
    return cut.transpose(0, 1, 3, 2, 4).reshape(
        shares, rows_by * columns_by, rows // rows_by, columns // columns_by
    )


def from_pieces(field, rows_by, columns_by):
    _, rows, columns = field.shape
    cut = field.reshape(rows_by, columns_by, rows, columns).transpose(0, 2, 1, 3)
    return cut.reshape(rows_by * rows, columns_by * columns)


DP_BITS = (1, 2, 4, 8)
ORDERS = ((0, 2, 3, 4), (2, 0, 3, 4), (3, 0, 2, 4), (0, 3, 4, 2))
SHARES = ((80, 384), (64, 384), (48, 576), (80, 384))
STEPS = 5


def stream_shapes(order, share):
    free = [0, 1, 2, 3, 4]
    boxes = []
    for dim in (1,) + order:
        free.remove(dim)
        boxes.append((2,) * len(free) + share)
    return boxes


def stream_scratch(streams):
    scratch = [pltpu.VMEM((2,) * 5 + SHARES[s], bf16) for s in streams]
    scratch += [pltpu.VMEM((2,) * 4 + SHARES[s], bf16) for s in streams]
    for s in streams:
        scratch += [pltpu.VMEM(box, bf16) for box in stream_shapes(ORDERS[s], SHARES[s])]
    return scratch + [pltpu.SemaphoreType.DMA((len(ORDERS), STEPS + 4))] * 2


def sum_streams(streams, ins, outs, scratch):
    gate_ref, up_ref, down_ref, attn_ref, slim_ref = ins
    q_out, k_out, v_out, o_out, gate_out, up_out, down_out, slim_out = outs
    count = len(streams)
    held = dict(zip(streams, scratch[:count]))
    result = dict(zip(streams, scratch[count : 2 * count]))
    boxes = {s: scratch[2 * count + i * STEPS :][:STEPS] for i, s in enumerate(streams)}
    send_sem, recv_sem = scratch[-2:]

    dp, fs = lax.axis_index("dp"), lax.axis_index("fsdp")
    mine = [fs] + [(dp // bit) % 2 for bit in DP_BITS]
    partner = [{"fsdp": 1 - fs}] + [
        {"dp": dp + bit - 2 * bit * own} for bit, own in zip(DP_BITS, mine[1:])
    ]

    barrier = pltpu.get_barrier_semaphore()
    for device in partner:
        pl.semaphore_signal(barrier, inc=1, device_id=device, device_id_type=pl.DeviceIdType.MESH)
    pl.semaphore_wait(barrier, len(partner))

    def copy(stream, step, source, target, dim):
        return pltpu.make_async_remote_copy(
            src_ref=source,
            dst_ref=target,
            send_sem=send_sem.at[stream, step],
            recv_sem=recv_sem.at[stream, step],
            device_id=partner[dim],
            device_id_type=pl.DeviceIdType.MESH,
        )

    def at(order, step, own_of_step):
        index = [slice(None)] * 5
        dims = (1,) + order
        for dim in dims[:step]:
            index[dim] = mine[dim]
        index[dims[step]] = own_of_step
        return tuple(index)

    def halve(stream, step):
        order = ORDERS[stream]
        dim = ((1,) + order)[step]
        index = at(order, step, 1 - mine[dim])
        return copy(stream, step, held[stream].at[index], boxes[stream][step], dim)

    def widen(stream, step):
        order = [dim for dim in ((1,) + ORDERS[stream])[::-1] if dim != 0]
        dim = order[step]
        index = [mine[at_dim] for at_dim in range(1, 5)]
        for done in order[:step]:
            index[done - 1] = slice(None)
        where = result[stream].at[tuple(index)]
        return copy(stream, STEPS + step, where, where, dim)

    def fill(stream):
        for f in range(2):
            for p in range(PIECES):
                c, x, zl, zh = p // 8, (p // 4) % 2, (p // 2) % 2, p % 2
                columns = slice((2 * zl + zh) * 384, (2 * zl + zh + 1) * 384)
                if stream < 2:
                    start = f * 288 + x * 144 + (80 if stream == 1 else 0)
                    source = up_ref if c else gate_ref
                    part = source[start : start + SHARES[stream][0], columns]
                elif stream == 2:
                    part = down_ref[f * 768 + p * 48 : f * 768 + p * 48 + 48, :]
                else:
                    start = f * 288 + (2 * c + x) * 72
                    part = jnp.concatenate(
                        [attn_ref[start : start + 72, columns], slim_ref[f, p]], axis=0
                    ).astype(bf16)
                held[stream][f, c, x, zl, zh] = part

    def empty(stream):
        for p in range(PIECES):
            c, x, zl, zh = p // 8, (p // 4) % 2, (p // 2) % 2, p % 2
            columns = slice((2 * zl + zh) * 384, (2 * zl + zh + 1) * 384)
            if stream == 3 and p % 4 != 0:
                continue
            part = result[stream][c, x, zl, zh].astype(f32)
            if stream < 2:
                start = x * 144 + (80 if stream == 1 else 0)
                target = up_out if c else gate_out
                target[start : start + SHARES[stream][0], columns] = part
            elif stream == 2:
                down_out[p * 48 : p * 48 + 48, :] = part
            else:
                quarters = [result[3][c, x, z // 2, z % 2].astype(f32) for z in range(4)]
                for z in range(4):
                    slim_out[p + z] = quarters[z][72:, :]
                row = jnp.concatenate([quarter[:72, :] for quarter in quarters], axis=1)
                rows = slice((p // 4) * 72, (p // 4) * 72 + 72)
                q_out[rows, :] = row[:, :D]
                k_out[rows, :] = row[:, D : D + KVW]
                v_out[rows, :] = row[:, D + KVW : QKV]
                o_out[rows, :] = row[:, QKV:]

    copies = {}
    for stream in streams:
        fill(stream)
        copies[stream] = halve(stream, 0)
        copies[stream].start()

    def narrow_step(step):
        for stream in streams:
            copies[stream].wait()
            order = ORDERS[stream]
            dim = ((1,) + order)[step]
            index = at(order, step, mine[dim])
            total = held[stream][index].astype(f32) + boxes[stream][step][...].astype(f32)
            if step < STEPS - 1:
                held[stream][index] = total.astype(bf16)
                copies[stream] = halve(stream, step + 1)
            else:
                result[stream][tuple(mine[1:])] = total.astype(bf16)
                copies[stream] = widen(stream, 0)
            copies[stream].start()

    def wide_step(step):
        for stream in streams:
            copies[stream].wait()
            if step < 3:
                copies[stream] = widen(stream, step + 1)
                copies[stream].start()
            else:
                empty(stream)

    left = [functools.partial(narrow_step, step) for step in range(STEPS)]
    return left + [functools.partial(wide_step, step) for step in range(4)]


FIRST, LAST = (0, 1, 2), (3,)


def backward_sum_kernel(*refs):
    attend_ins, (gate, up, down) = refs[:10], refs[10:13]
    out_ref, outs = refs[13], refs[14:17]
    own = len(backward_scratch())
    left = sum_streams(
        FIRST, (gate, up, down, None, None), (None,) * 4 + outs + (None,), refs[17 + own :]
    )

    def between(block, kv):
        if (block, kv) in ((3, 0), (3, 2), (2, 1), (1, 0), (1, 2), (0, 2)):
            left.pop(0)()

    backward_kernel(*attend_ins, out_ref, *refs[17 : 17 + own], between=between)
    for step in left:
        step()


def attend_backward_sum(parts, grads):
    shapes = [(288, 1536), (288, 1536), (768, D)]
    return pl.pallas_call(
        backward_sum_kernel,
        out_shape=(jax.ShapeDtypeStruct((HEADS + 2 * KV_HEADS, HEAD_DIM, SEQ), bf16),)
        + tuple(jax.ShapeDtypeStruct(shape, f32) for shape in shapes),
        in_specs=vmem(13),
        out_specs=tuple(vmem(4)),
        scratch_shapes=backward_scratch() + stream_scratch(FIRST),
        compiler_params=pltpu.CompilerParams(
            collective_id=0, has_side_effects=True, vmem_limit_bytes=56 << 20
        ),
    )(*parts, *grads)


def last_kernel(*refs):
    ins, outs = (None,) * 3 + refs[:2], refs[2:6] + (None,) * 3 + refs[6:7]
    for step in sum_streams(LAST, ins, outs, refs[7:]):
        step()


def sum_last(attn, slim):
    shapes = [(288, D), (288, KVW), (288, KVW), (288, D), (PIECES, 8, 384)]
    return pl.pallas_call(
        last_kernel,
        out_shape=tuple(jax.ShapeDtypeStruct(shape, f32) for shape in shapes),
        in_specs=vmem(2),
        out_specs=tuple(vmem(5)),
        scratch_shapes=stream_scratch(LAST),
        compiler_params=pltpu.CompilerParams(
            collective_id=1, has_side_effects=True, vmem_limit_bytes=48 << 20
        ),
    )(attn, slim)


def on_device(
    sizes,
    tokens,
    segments,
    w_query,
    w_key,
    w_value,
    w_out,
    w_gate,
    w_up,
    w_down,
    gain_attn,
    gain_ffn,
    cotangent,
):
    dp, fs = lax.axis_index("dp"), lax.axis_index("fsdp")
    count = tokens.shape[0]
    seq_count = count // SEQ
    shard_d = w_query.shape[0]

    gains = jnp.concatenate(
        [gain_attn[:, None], gain_ffn[:, None], jnp.zeros((shard_d, 62), bf16)], axis=1
    )
    first = jnp.concatenate([w_query, w_key, w_value, gains], axis=1)
    first_full = gather_full(first, dp, fs, sizes)
    w_qkv = first_full[:, :QKV]
    ga_full = first_full[:, QKV].astype(f32)
    gf_full = first_full[:, QKV + 1].astype(f32)
    later, _ = lax.optimization_barrier(((w_out, w_gate, w_up, w_down), first_full))
    wo_full, wg_full, wu_full, wd_full = [gather_full(w, dp, fs, sizes) for w in later]

    positions = positions_of(segments)
    freqs = rope_base ** (-jnp.arange(0, HEAD_DIM, 2).astype(f32) / HEAD_DIM)
    phase = freqs[:, None] * positions.astype(f32)[None, :]
    cosine, sine = jnp.cos(phase), jnp.sin(phase)

    tok_float = tokens.astype(f32)
    scale_attn = rms_scale(tok_float)
    normed_attn = tok_float * scale_attn
    hidden_attn = (normed_attn * ga_full).astype(bf16)
    raw = lax.dot_general(
        w_qkv, hidden_attn, (((0,), (1,)), ((), ())), preferred_element_type=f32
    )
    spans = [slice(s * SEQ, (s + 1) * SEQ) for s in range(seq_count)]
    seg_cols = [segments[span].reshape(SEQ, 1) for span in spans]
    seg_rows = [segments[span].reshape(1, SEQ) for span in spans]
    kept = [
        attend_forward(raw[:, span], cosine[:, span], sine[:, span], col, row)
        for span, col, row in zip(spans, seg_cols, seg_rows)
    ]
    join = lambda parts: parts[0] if len(parts) == 1 else jnp.concatenate(parts, axis=-1)
    mixed = join([part[3].reshape(D, SEQ) for part in kept])
    middle = tok_float + dot_t(mixed, wo_full)
    scale_ffn = rms_scale(middle)
    normed_ffn = middle * scale_ffn
    hidden_ffn = (normed_ffn * gf_full).astype(bf16)
    gate = mm(hidden_ffn, wg_full)
    upward = mm(hidden_ffn, wu_full)
    sigmoid_gate = jax.nn.sigmoid(gate)
    silu_gate = gate * sigmoid_gate
    inner = (silu_gate * upward).astype(bf16)
    output = (middle + mm(inner, wd_full)).astype(bf16)

    grad_down = dot_t(inner, cotangent).astype(bf16)
    grad_inner = jnp.einsum("td,fd->tf", cotangent, wd_full, preferred_element_type=f32)
    grad_gate_act = (
        grad_inner * upward * sigmoid_gate * (1.0 + gate * (1.0 - sigmoid_gate))
    ).astype(bf16)
    grad_upward = (grad_inner * silu_gate).astype(bf16)
    grad_gate = dot_t(hidden_ffn, grad_gate_act).astype(bf16)
    grad_up = dot_t(hidden_ffn, grad_upward).astype(bf16)
    grad_hidden_ffn = jnp.einsum(
        "tf,df->td", grad_gate_act, wg_full, preferred_element_type=f32
    ) + jnp.einsum("tf,df->td", grad_upward, wu_full, preferred_element_type=f32)
    grad_gain_ffn = jnp.sum(grad_hidden_ffn * normed_ffn, axis=0)
    grad_normed_ffn = grad_hidden_ffn * gf_full
    grad_middle = cotangent.astype(f32) + scale_ffn * (
        grad_normed_ffn - normed_ffn * jnp.mean(grad_normed_ffn * normed_ffn, axis=1, keepdims=True)
    )
    grad_branch = grad_middle.astype(bf16)

    grad_out = mm(mixed, grad_branch)
    grad_mixed = lax.dot_general(
        wo_full, grad_branch, (((1,), (1,)), ((), ())), preferred_element_type=f32
    ).astype(bf16)
    backs = [
        (*part, grad_mixed[:, span].reshape(HEADS, HEAD_DIM, SEQ),
         cosine[:, span], sine[:, span], col, row)
        for part, span, col, row in zip(kept, spans, seg_cols, seg_rows)
    ]
    fused = sizes == (16, 2) and seq_count == 1
    if fused:
        grad_raw, *ffn_sums = attend_backward_sum(backs[0], (grad_gate, grad_up, grad_down))
        grad_raw = grad_raw.reshape(QKV, SEQ)
    else:
        grad_raw = join([attend_backward(*back).reshape(QKV, SEQ) for back in backs])
    grad_qkv = lax.dot_general(
        hidden_attn, grad_raw, (((0,), (1,)), ((), ())), preferred_element_type=f32
    )
    grad_hidden_attn = lax.dot_general(
        grad_raw, w_qkv, (((0,), (1,)), ((), ())), preferred_element_type=f32
    )
    grad_gain_attn = jnp.sum(grad_hidden_attn * normed_attn, axis=0)
    grad_normed_attn = grad_hidden_attn * ga_full
    grad_tokens = grad_middle + scale_attn * (
        grad_normed_attn
        - normed_attn * jnp.mean(grad_normed_attn * normed_attn, axis=1, keepdims=True)
    )

    wide = jnp.concatenate([grad_qkv, grad_out], axis=1)
    slim = jnp.stack([grad_gain_attn, grad_gain_ffn]).reshape(2, sizes[1], shard_d).swapaxes(0, 1)
    slim = slim.reshape(sizes[1], PIECES, 1, 2 * shard_d // PIECES)
    slim = jnp.pad(slim, ((0, 0), (0, 0), (0, 7), (0, wide.shape[1] // 4 - slim.shape[3])))
    slim_width = 2 * shard_d // PIECES
    if fused:
        *sums, slim_sum = sum_last(wide, slim)
        sums = sums + ffn_sums
        slim_sum = slim_sum[:, 0, :slim_width].reshape(2, shard_d)
        return (output, grad_tokens.astype(bf16), *sums, slim_sum[0], slim_sum[1])

    pieces = lambda field, *by: as_pieces(field, sizes[1], *by)
    reduce = functools.partial(reduce_pieces, dp=dp, fs=fs, sizes=sizes)
    gate_up_sum = reduce(
        jnp.concatenate([pieces(grad_gate, 2, 4), pieces(grad_up, 2, 4)], axis=1)
    )
    down_sum = reduce(pieces(grad_down, PIECES, 1))
    wide = pieces(wide.astype(bf16), 4, 4)
    attn_sum = reduce(jnp.concatenate([wide, slim.astype(bf16)], axis=2))
    rows = wide.shape[2]
    wide_sum = from_pieces(attn_sum[:, :rows], 4, 4).astype(f32)
    slim_sum = attn_sum[:, rows, :slim_width].reshape(2, shard_d).astype(f32)
    return (
        output,
        grad_tokens.astype(bf16),
        wide_sum[:, :D],
        wide_sum[:, D : D + KVW],
        wide_sum[:, D + KVW : QKV],
        wide_sum[:, QKV:],
        from_pieces(gate_up_sum[: PIECES // 2], 2, 4).astype(f32),
        from_pieces(gate_up_sum[PIECES // 2 :], 2, 4).astype(f32),
        from_pieces(down_sum, PIECES, 1).astype(f32),
        slim_sum[0],
        slim_sum[1],
    )


def solution(mesh):
    rows, whole = P(("dp", "fsdp"), None), P(("dp", "fsdp"))
    weight, gain = P("fsdp", None), P("fsdp")
    in_specs = (rows, whole) + (weight,) * 7 + (gain, gain, rows)
    out_specs = (rows, rows) + (weight,) * 7 + (gain, gain)
    sizes = (mesh.shape["dp"], mesh.shape["fsdp"])
    return jax.shard_map(
        functools.partial(on_device, sizes),
        mesh=mesh,
        in_specs=in_specs,
        out_specs=out_specs,
        check_vma=False,
    )
```
